32 devices in a mesh: grp: 2 (over y), obs: 4 (over z), par: 4 (over x, core).
Axes of the slice: x: 2, y: 2, z: 4, core: 2. Of those that a mesh axis runs over, the one named last changes fastest.
Arguments:
- predicted: bfloat16 [256, 786432], P(None, ('grp', 'obs', 'par')), parts along dimension 1, may hold values from -120 to 120
- observed: float32 [786432], P(('grp', 'obs', 'par')), parts along dimension 0, may hold values from -120 to 120
- band: float32 [8, 786432], P(None, ('grp', 'obs', 'par')), parts along dimension 1, may hold values from -5 to 5
- offsets: int32 [8], replicated, may hold values from -1024 to 1024, as said below
- rows_count: int32 [32], P(('grp', 'obs', 'par')), parts along dimension 0, may hold values from 12288 to 23552, as said below
- params: bfloat16 [16384, 256], P(('grp', 'obs', 'par')), parts along dimension 0, may hold values from -6 to 6
Outputs:
- params_new: float32 [16384, 256], P(('grp', 'obs', 'par')), parts along dimension 0
- whitened_misfit: float32 [786432], P(('grp', 'obs', 'par')), parts along dimension 0
The draws below stay inside these ranges and needn't reach their ends.
There are 2 independent parts, one for each index of `grp`. The reference program is written for one: setup_inputs(seed, part) draws one part's arguments, and reference() takes and returns one part's arrays. A program takes and returns all parts, laid end to end along the dimension named above; an argument that names none is the same for every part. Nothing has to cross between parts.
Inputs may be any that keep to these rules, and one draw needn't show every extreme that they name: offsets[0] is 0, the 8 offsets are distinct, and both -1024 and 1024 are among them. `rows_count`: every shard holds this many strain observations first, then load observations up to its last 1024 observations, which are strain observations again; in every draw some shard holds exactly 23552 leading strain observations and some exactly 12288.
All inputs are finite; a program needn't handle non-finite values.
Results may differ from the reference program's by a relative error of at most 0.0029.
Values may be sent and summed in bfloat16 or wider, within the bound.
A program may use at most 256 MiB of HBM per device.

```python
import math
import jax
import jax.numpy as jnp
from jax import lax

M = 256
B = 8
H = 1024
O_DEV = 24576
SHARDS = 16
NOBS = 393216
NPAR = 8192


def shared_parts(key):
    shared = jax.random.normal(jax.random.fold_in(key, 11), (M // 8, NOBS), jnp.float32)
    row_ramp = jnp.arange(NOBS, dtype=jnp.float32) * (math.log(3.0) / NOBS)
    row_scale = jnp.exp(jax.random.uniform(jax.random.fold_in(key, 12), (NOBS,), jnp.float32, -0.8, 0.8) + row_ramp)
    groups = jax.random.permutation(jax.random.fold_in(key, 13), M) // 8
    member_scale = jnp.exp(jax.random.uniform(jax.random.fold_in(key, 14), (M,), jnp.float32, -1.15, 1.15))
    return (shared, row_scale, groups, member_scale)


def draw_predicted(key, part):
    shared, row_scale, groups, member_scale = shared_parts(key)
    noise = jax.random.normal(jax.random.fold_in(key, 21), (M, NOBS), jnp.float32)
    common = shared[groups]
    values = member_scale[:, None] * row_scale[None, :] * (noise + common)
    return jnp.clip(values, -120.0, 120.0).astype(jnp.bfloat16)


def draw_observed(key, part):
    shared, row_scale, groups, member_scale = shared_parts(key)
    noise = jax.random.normal(jax.random.fold_in(key, 31), (NOBS,), jnp.float32)
    values = row_scale * (0.7 * shared[0] + 0.7 * shared[1] + noise)
    return jnp.clip(values, -120.0, 120.0)


def draw_offsets(key, part):
    others = jnp.concatenate([jnp.arange(1 - H, 0, dtype=jnp.int32), jnp.arange(1, H, dtype=jnp.int32)])
    picked = jax.random.permutation(jax.random.fold_in(key, 41), others)[:B - 3]
    rest_values = jnp.concatenate([jnp.array([H, -H], dtype=jnp.int32), picked])
    rest_values = jax.random.permutation(jax.random.fold_in(key, 42), rest_values)
    return jnp.concatenate([jnp.zeros((1,), jnp.int32), rest_values])


def draw_rows_count(key, part):
    counts_drawn = jax.random.randint(jax.random.fold_in(key, 51), (SHARDS,), O_DEV // 2, O_DEV - H + 1, dtype=jnp.int32)
    full_at = jax.random.randint(jax.random.fold_in(key, 52), (), 0, SHARDS, dtype=jnp.int32)
    half_at = (full_at + 1 + jax.random.randint(jax.random.fold_in(key, 53), (), 0, SHARDS - 1, dtype=jnp.int32)) % SHARDS
    counts_drawn = counts_drawn.at[full_at].set(O_DEV - H)
    counts_drawn = counts_drawn.at[half_at].set(O_DEV // 2)
    return counts_drawn


def shard_levels(key, dims, split, low, top_value):
    gain, own = 1.0, jax.random.fold_in(key, 6)
    for dim, blocks in split:
        heights = jnp.exp(jax.random.uniform(jax.random.fold_in(own, dim), (blocks,), jnp.float32, low / len(split), top_value / len(split)))
        gain = gain * jnp.repeat(heights, dims[dim] // blocks).reshape([-1 if axis == dim else 1 for axis in range(len(dims))])
    return gain


def centred(key, shape, deviation, reach, shards=(), held_as=jnp.bfloat16):
    level = shard_levels(key, shape, shards, -0.22, 0.18) if shards else 1.0
    drawn = jax.random.normal(key, shape, jnp.float32) * deviation * level
    return jnp.minimum(jnp.maximum(drawn, -reach), reach).astype(held_as)


def setup_inputs(seed: int = 0, part: int = 0) -> dict:
    key_list = jax.random.split(jax.random.key(seed), 7)
    own_keys = jax.random.split(jax.random.fold_in(key_list[6], part), 7)
    predicted = draw_predicted(jax.random.fold_in(jax.random.fold_in(key_list[6], part), 71), part)
    observed = draw_observed(jax.random.fold_in(jax.random.fold_in(key_list[6], part), 71), part)
    band = centred(own_keys[2], (B, NOBS), 0.35, 5.0, ((1, 16),), jnp.float32)
    offsets = draw_offsets(jax.random.fold_in(key_list[6], 71), part)
    rows_count = draw_rows_count(jax.random.fold_in(jax.random.fold_in(key_list[6], part), 71), part)
    params = centred(own_keys[5], (NPAR, M), 1.0, 6.0, ((0, 16),))
    return {"predicted": predicted, "observed": observed, "band": band, "offsets": offsets, "rows_count": rows_count, "params": params}


def whiten(padded, band_block, offsets, strain):
    columns = band_block.shape[1]

    def shifted(term):
        begin = (H + offsets[term]).astype(jnp.int32)
        return lax.dynamic_slice_in_dim(padded, begin, columns, 1).astype(jnp.float32)
    leading = band_block[0] * shifted(0)
    extra_terms = jnp.zeros_like(leading)
    for term in range(1, B):
        extra_terms = extra_terms + band_block[term] * shifted(term)
    return leading + strain * extra_terms

def reference(predicted, observed, band, offsets, rows_count, params):
    obs_total = O_DEV * SHARDS
    row_factor = 1.0 / math.sqrt(obs_total)
    misfit_factor = math.sqrt((M - 1) / obs_total)
    pred_pad = jnp.pad(predicted, ((0, 0), (H, H)))
    obs_pad = jnp.pad(observed, (H, H))

    def shard_step(carry, shard):
        gram_total, projection = carry
        offset_at = (shard * O_DEV).astype(jnp.int32)
        pred_block = lax.dynamic_slice_in_dim(pred_pad, offset_at, O_DEV + 2 * H, 1).astype(jnp.float32)
        obs_block = lax.dynamic_slice_in_dim(obs_pad, offset_at, O_DEV + 2 * H, 0)
        mean_pred = lax.optimization_barrier(jnp.mean(pred_block, axis=0))
        anomaly = lax.optimization_barrier((pred_block - mean_pred).astype(jnp.bfloat16))
        innovation = lax.optimization_barrier((obs_block - mean_pred).astype(jnp.bfloat16))
        joint = jnp.concatenate([innovation[None, :], anomaly], 0)
        band_block = lax.dynamic_slice_in_dim(band, offset_at, O_DEV, 1)
        local_index = lax.iota(jnp.int32, O_DEV)
        strain = ((local_index < rows_count[shard]) | (local_index >= O_DEV - H)).astype(jnp.float32)
        whitened = whiten(joint, band_block, offsets, strain)
        anomaly_white = (whitened[1:] * row_factor).astype(jnp.bfloat16)
        misfit = whitened[0] * misfit_factor
        gram_total = gram_total + lax.dot_general(anomaly_white.astype(jnp.float32), anomaly_white.astype(jnp.float32), (((1,), (1,)), ((), ())), preferred_element_type=jnp.float32)
        projection = projection + jnp.dot(anomaly_white.astype(jnp.float32), misfit, precision=lax.Precision.HIGHEST)
        return ((gram_total, projection), misfit)
    initial = (jnp.zeros((M, M), jnp.float32), jnp.zeros((M,), jnp.float32))
    (gram_total, projection), misfits = lax.scan(shard_step, initial, jnp.arange(SHARDS, dtype=jnp.int32))
    whitened_misfit = misfits.reshape(SHARDS * O_DEV)
    identity = jnp.eye(M, dtype=jnp.float32)
    lower_factor = jnp.linalg.cholesky(identity + gram_total)
    weights = jax.scipy.linalg.cho_solve((lower_factor, True), projection)
    inverse_t = jax.scipy.linalg.solve_triangular(lower_factor, identity, lower=True).T
    transform = weights[:, None] / math.sqrt(M - 1) + inverse_t
    params_wide = params.astype(jnp.float32)
    param_mean = lax.optimization_barrier(jnp.mean(params_wide, axis=1, keepdims=True))
    params_new = param_mean + jnp.dot(params_wide - param_mean, transform, precision=lax.Precision.HIGHEST)
    return (params_new, whitened_misfit)
```

```python
import functools
import math

import jax
import jax.numpy as jnp
from jax import lax
from jax.experimental import pallas as pl
from jax.experimental.pallas import tpu as pltpu
from jax.sharding import PartitionSpec as P

H = 1024
LANES = 128
ROWS = 32
EXTRA = 16
BLOCK = 32
MESH = pl.DeviceIdType.MESH


def whiten_kernel(
    tiles, off_ref, count_ref, pred_ref, left_ref, right_ref, obs_ref, obs_left_ref, obs_right_ref, band_ref,
    acc_ref, misfit_ref, anomaly, innovation, coef, white,
):
    step = pl.program_id(0)
    members = pred_ref.shape[0]
    terms = band_ref.shape[0]

    def enter(pred, obs):
        wide = pred.astype(jnp.float32)
        mean = jnp.sum(wide, axis=0, keepdims=True) * (1.0 / members)
        at = pl.ds(pl.multiple_of(step * H, H), H)
        anomaly[:, at] = (wide - mean).astype(jnp.bfloat16)
        innov = (obs - mean).astype(jnp.bfloat16).astype(jnp.float32)
        innovation[:, at] = jnp.broadcast_to(innov, (8, H))

    @pl.when(step == 0)
    def _():
        enter(left_ref[...], obs_left_ref[...])
        acc_ref[...] = jnp.zeros_like(acc_ref)

    @pl.when((step > 0) & (step <= tiles))
    def _():
        enter(pred_ref[...], obs_ref[...])

    @pl.when(step == tiles + 1)
    def _():
        enter(right_ref[...], obs_right_ref[...])

    @pl.when(step >= 2)
    def _():
        tile = step - 2
        local = tile * H + lax.broadcasted_iota(jnp.int32, (1, H), 1)
        strain = ((local < count_ref[0]) | (local >= (tiles - 1) * H)).astype(jnp.float32)
        lane = lax.broadcasted_iota(jnp.int32, (ROWS, LANES), 1)
        lane8 = lax.broadcasted_iota(jnp.int32, (8, LANES), 1)
        starts, shifts, cuts = [], [], []
        for k in range(terms):
            begin = (tile + 1) * H + off_ref[k]
            rest = lax.rem(begin, LANES)
            starts.append(begin - rest)
            shifts.append(lax.rem(LANES - rest, LANES))
            cuts.append(LANES - rest)
        pieces = H // LANES
        row_sum = [None] * pieces
        for k in range(terms):
            factor = band_ref[k : k + 1, :]
            if k:
                factor = factor * strain
            coef[k] = jnp.broadcast_to(factor, (ROWS, H)).astype(jnp.bfloat16)
            rolled = [
                pltpu.roll(
                    innovation[:, pl.ds(pl.multiple_of(starts[k] + j * LANES, LANES), LANES)], shifts[k], 1
                )
                for j in range(pieces + 1)
            ]
            for j in range(pieces):
                part = jnp.where(lane8 < cuts[k], rolled[j], rolled[j + 1])[0:1, :]
                part = part * factor[:, j * LANES : (j + 1) * LANES]
                row_sum[j] = part if k == 0 else row_sum[j] + part
        row = jnp.concatenate(row_sum, axis=1)
        misfit_ref[...] = row
        high = row.astype(jnp.bfloat16).astype(jnp.float32)
        which = lax.broadcasted_iota(jnp.int32, (EXTRA, H), 0)
        extra = jnp.where(which == 0, high, jnp.where(which == 1, row - high, 0.0))
        white[members : members + EXTRA, :] = extra.astype(jnp.bfloat16)

        def rows(chunk, carry):
            here = pl.ds(pl.multiple_of(chunk * ROWS, ROWS), ROWS)
            sums = [None] * pieces
            for k in range(terms):
                before = None
                for j in range(pieces + 1):
                    block = anomaly[here, pl.ds(pl.multiple_of(starts[k] + j * LANES, LANES), LANES)]
                    rolled = pltpu.roll(block.astype(ROLL), shifts[k], 1)
                    if j:
                        part = jnp.where(lane < cuts[k], before, rolled).astype(ACC)
                        part = part * coef[k, :, (j - 1) * LANES : j * LANES].astype(ACC)
                        sums[j - 1] = part if k == 0 else sums[j - 1] + part
                    before = rolled
            for j in range(pieces):
                white[here, j * LANES : (j + 1) * LANES] = sums[j].astype(jnp.bfloat16)
            return carry

        lax.fori_loop(0, members // ROWS, rows, 0)
        acc_ref[...] += lax.dot_general(
            white[...], white[0:members, :], (((1,), (1,)), ((), ())), preferred_element_type=jnp.float32
        )


ROLL = jnp.bfloat16
ACC = jnp.bfloat16


def whiten_gram(offsets, count, predicted, left, right, observed, obs_left, obs_right, band):
    members, columns = predicted.shape
    terms = band.shape[0]
    tiles = columns // H
    smem = pl.BlockSpec(memory_space=pltpu.SMEM)
    enter = lambda s: (0, jnp.clip(s - 1, 0, tiles - 1))
    leave = lambda s: (0, jnp.clip(s - 2, 0, tiles - 1))
    fixed = lambda s: (0, 0)
    return pl.pallas_call(
        functools.partial(whiten_kernel, tiles),
        grid=(tiles + 2,),
        out_shape=(
            jax.ShapeDtypeStruct((members + EXTRA, members), jnp.float32),
            jax.ShapeDtypeStruct((1, columns), jnp.float32),
        ),
        in_specs=[
            smem, smem,
            pl.BlockSpec((members, H), enter),
            pl.BlockSpec((members, H), fixed),
            pl.BlockSpec((members, H), fixed),
            pl.BlockSpec((1, H), enter),
            pl.BlockSpec((1, H), fixed),
            pl.BlockSpec((1, H), fixed),
            pl.BlockSpec((terms, H), leave),
        ],
        out_specs=(
            pl.BlockSpec((members + EXTRA, members), fixed),
            pl.BlockSpec((1, H), leave),
        ),
        scratch_shapes=[
            pltpu.VMEM((members, columns + 2 * H + LANES), jnp.bfloat16),
            pltpu.VMEM((8, columns + 2 * H + LANES), jnp.float32),
            pltpu.VMEM((terms, ROWS, H), jnp.bfloat16),
            pltpu.VMEM((members + EXTRA, H), jnp.bfloat16),
        ],
        compiler_params=pltpu.CompilerParams(vmem_limit_bytes=48 << 20),
    )(offsets, count, predicted, left, right, observed, obs_left, obs_right, band)


def sum_kernel(shards, x_ref, out_ref, arrived, chunks, send_a, recv_a, send_b, recv_b):
    lines = arrived.shape[1]
    grp = lax.axis_index("grp")
    par_size = lax.axis_size("par")
    me = lax.axis_index("obs") * par_size + lax.axis_index("par")

    def where(d):
        peer = lax.rem(me + d, shards)
        return peer, (grp, peer // par_size, lax.rem(peer, par_size))

    barrier = pltpu.get_barrier_semaphore()
    for d in range(1, shards):
        pl.semaphore_signal(barrier, inc=1, device_id=where(d)[1], device_id_type=MESH)
    pl.semaphore_wait(barrier, shards - 1)
    first = []
    for d in range(1, shards):
        peer, device = where(d)
        copy = pltpu.make_async_remote_copy(
            src_ref=x_ref.at[peer], dst_ref=arrived.at[d],
            send_sem=send_a.at[d], recv_sem=recv_a.at[d], device_id=device, device_id_type=MESH,
        )
        copy.start()
        first.append(copy)
    total = x_ref[me]
    for d in range(1, shards):
        first[d - 1].wait()
        total = total + arrived[d]
    proj = total[lines - 8 : lines, :]
    chunks[...] = total[0 : lines - 8, :]
    size = lines - 8
    mine = pl.ds(pl.multiple_of(me * size, size), size)
    second = []
    for d in range(1, shards):
        peer, device = where(d)
        copy = pltpu.make_async_remote_copy(
            src_ref=chunks, dst_ref=out_ref.at[mine],
            send_sem=send_b.at[d], recv_sem=recv_b.at[d], device_id=device, device_id_type=MESH,
        )
        copy.start()
        second.append(copy)
    out_ref[mine, :] = chunks[...]
    out_ref[shards * size : shards * size + 8, :] = proj
    for d in range(1, shards):
        second[d - 1].wait()


def sum_over_shards(acc, shards):
    members = acc.shape[1]
    if shards > 1 and members % shards == 0 and (members // shards) % 8 == 0:
        size = members // shards
        chunks = acc[:members].reshape(shards, size, members)
        tail = jnp.broadcast_to(acc[members : members + 8][None], (shards, 8, members))
        vmem = pl.BlockSpec(memory_space=pltpu.VMEM)
        return pl.pallas_call(
            functools.partial(sum_kernel, shards),
            out_shape=jax.ShapeDtypeStruct((members + 8, members), jnp.float32),
            in_specs=[vmem],
            out_specs=vmem,
            scratch_shapes=[
                pltpu.VMEM((shards, size + 8, members), jnp.float32),
                pltpu.VMEM((size, members), jnp.float32),
                pltpu.SemaphoreType.DMA((shards,)),
                pltpu.SemaphoreType.DMA((shards,)),
                pltpu.SemaphoreType.DMA((shards,)),
                pltpu.SemaphoreType.DMA((shards,)),
            ],
            compiler_params=pltpu.CompilerParams(collective_id=0, has_side_effects=True),
        )(jnp.concatenate([chunks, tail], axis=1))
    return lax.psum(acc[: members + 8], ("obs", "par"))


def exact(a, b, dims):
    return lax.dot_general(
        a, b, (dims, ((), ())), precision=lax.Precision.HIGHEST, preferred_element_type=jnp.float32
    )


def transform_kernel(obs_total, x_ref, out_ref, left, right):
    members = out_ref.shape[0]
    scale = 1.0 / obs_total
    line = lax.broadcasted_iota(jnp.int32, (members, members), 0)
    column = lax.broadcasted_iota(jnp.int32, (members, members), 1)
    eye = (line == column).astype(jnp.float32)
    left[...] = x_ref[0:members, :] * scale + eye
    right[...] = eye
    small_line = lax.broadcasted_iota(jnp.int32, (BLOCK, 1), 0)
    small = (
        lax.broadcasted_iota(jnp.int32, (BLOCK, BLOCK), 0) == lax.broadcasted_iota(jnp.int32, (BLOCK, BLOCK), 1)
    ).astype(jnp.float32)
    for b in range(members // BLOCK):
        lo, hi = b * BLOCK, (b + 1) * BLOCK
        a = left[lo:hi, lo:hi]
        x = small
        for j in range(BLOCK):
            factor = a[:, j : j + 1] / a[j : j + 1, j : j + 1]
            factor = jnp.where(small_line > j, factor, 0.0)
            x = x - factor * x[j : j + 1, :]
            a = a - factor * a[j : j + 1, :]
        diagonal = jnp.sum(a * small, axis=1, keepdims=True)
        x = x * lax.rsqrt(diagonal)
        panel_left = exact(x, left[lo:hi, :], ((1,), (0,)))
        panel_right = exact(x, right[lo:hi, :], ((1,), (0,)))
        right[lo:hi, :] = panel_right
        if hi < members:
            outer = panel_left
            update_left = exact(outer, panel_left, ((0,), (0,)))
            update_right = exact(outer, panel_right, ((0,), (0,)))
            left[hi:, :] = left[hi:, :] - update_left[hi:, :]
            right[hi:, :] = right[hi:, :] - update_right[hi:, :]
    inverse = right[...]
    projection = (x_ref[members : members + 1, :] + x_ref[members + 1 : members + 2, :]) * (
        math.sqrt(members - 1) / obs_total
    )
    half = jnp.sum(inverse * projection, axis=1, keepdims=True)
    weights = exact(inverse, jnp.broadcast_to(half, (members, LANES)), ((0,), (0,)))[:, 0:1]
    out_ref[...] = inverse.T + weights * (1.0 / math.sqrt(members - 1))


def transform_of(total, obs_total):
    members = total.shape[1]
    return pl.pallas_call(
        functools.partial(transform_kernel, obs_total),
        out_shape=jax.ShapeDtypeStruct((members, members), jnp.float32),
        scratch_shapes=[pltpu.VMEM((members, members), jnp.float32)] * 2,
        compiler_params=pltpu.CompilerParams(vmem_limit_bytes=32 << 20),
    )(total)


def body(predicted, observed, band, offsets, rows_count, params):
    members = predicted.shape[0]
    columns = predicted.shape[1]
    axes = ("obs", "par")
    shards = lax.axis_size(axes)
    obs_total = columns * shards
    misfit_factor = math.sqrt((members - 1) / obs_total)
    up = [(i, i + 1) for i in range(shards - 1)]
    down = [(j, i) for i, j in up]
    obs_row = observed[None, :]
    left = lax.ppermute(predicted[:, columns - H :], axes, up)
    right = lax.ppermute(predicted[:, :H], axes, down)
    obs_left = lax.ppermute(obs_row[:, columns - H :], axes, up)
    obs_right = lax.ppermute(obs_row[:, :H], axes, down)
    acc, row = whiten_gram(
        offsets, rows_count, predicted, left, right, obs_row, obs_left, obs_right, band
    )
    total = sum_over_shards(acc, shards)
    transform = transform_of(total, obs_total)
    params_wide = params.astype(jnp.float32)
    param_mean = jnp.mean(params_wide, axis=1, keepdims=True)
    params_new = param_mean + jnp.dot(
        params_wide - param_mean, transform, precision=lax.Precision.HIGHEST
    )
    return (params_new, row[0] * misfit_factor)


def solution(mesh):
    in_specs = (
        P(None, ("grp", "obs", "par")),
        P(("grp", "obs", "par")),
        P(None, ("grp", "obs", "par")),
        P(),
        P(("grp", "obs", "par")),
        P(("grp", "obs", "par"), None),
    )
    out_specs = (P(("grp", "obs", "par"), None), P(("grp", "obs", "par")))
    return jax.shard_map(body, mesh=mesh, in_specs=in_specs, out_specs=out_specs, check_vma=False)
```

```python
import functools
import math

import jax
import jax.numpy as jnp
from jax import lax
from jax.experimental import pallas as pl
from jax.experimental.pallas import tpu as pltpu
from jax.sharding import PartitionSpec as P

H = 1024
LANES = 128
ROWS = 64
EXTRA = 16
BLOCK = 32
MESH = pl.DeviceIdType.MESH


def whiten_kernel(
    tiles, off_ref, count_ref, pred_ref, left_ref, right_ref, obs_ref, band_ref,
    acc_ref, misfit_ref, anomaly, innovation, coef, white,
):
    step = pl.program_id(0)
    members = pred_ref.shape[0]
    terms = band_ref.shape[0]

    def enter(pred, obs):
        wide = pred.astype(jnp.float32)
        mean = jnp.sum(wide, axis=0, keepdims=True) * (1.0 / members)
        at = pl.ds(pl.multiple_of(step * H, H), H)
        anomaly[:, at] = (wide - mean).astype(jnp.bfloat16)
        innov = (obs - mean).astype(jnp.bfloat16).astype(jnp.float32)
        innovation[:, at] = jnp.broadcast_to(innov, (8, H))

    def unpack(ref):
        parts = ref[members : members + EXTRA, :].astype(jnp.float32)
        return ref[0:members, :], parts[0:1, :] + (parts[1:2, :] + parts[2:3, :])

    @pl.when(step == 0)
    def _():
        enter(*unpack(left_ref))
        acc_ref[...] = jnp.zeros_like(acc_ref)

    @pl.when((step > 0) & (step <= tiles))
    def _():
        enter(pred_ref[...], obs_ref[...])

    @pl.when(step == tiles + 1)
    def _():
        enter(*unpack(right_ref))

    @pl.when(step >= 2)
    def _():
        tile = step - 2
        local = tile * H + lax.broadcasted_iota(jnp.int32, (1, H), 1)
        strain = ((local < count_ref[0]) | (local >= (tiles - 1) * H)).astype(jnp.float32)
        lane = lax.broadcasted_iota(jnp.int32, (16, LANES), 1)
        lane8 = lax.broadcasted_iota(jnp.int32, (8, LANES), 1)
        starts, shifts, cuts = [], [], []
        for k in range(terms):
            begin = (tile + 1) * H + off_ref[k]
            rest = lax.rem(begin, LANES)
            starts.append(begin - rest)
            shifts.append(lax.rem(LANES - rest, LANES))
            cuts.append(LANES - rest)
        pieces = H // LANES
        row_sum = [None] * pieces
        for k in range(terms):
            factor = band_ref[k : k + 1, :]
            if k:
                factor = factor * strain
            coef[k] = jnp.broadcast_to(factor.astype(jnp.bfloat16), (16, H))
            rolled = [
                pltpu.roll(
                    innovation[:, pl.ds(pl.multiple_of(starts[k] + j * LANES, LANES), LANES)], shifts[k], 1
                )
                for j in range(pieces + 1)
            ]
            for j in range(pieces):
                part = jnp.where(lane8 < cuts[k], rolled[j], rolled[j + 1])[0:1, :]
                part = part * factor[:, j * LANES : (j + 1) * LANES]
                row_sum[j] = part if k == 0 else row_sum[j] + part
        row = jnp.concatenate(row_sum, axis=1)
        misfit_ref[...] = row
        high = row.astype(jnp.bfloat16).astype(jnp.float32)
        which = lax.broadcasted_iota(jnp.int32, (EXTRA, H), 0)
        extra = jnp.where(which == 0, high, jnp.where(which == 1, row - high, 0.0))
        white[members : members + EXTRA, :] = extra.astype(jnp.bfloat16)

        keep = [lane < cut for cut in cuts]

        def rows(chunk, carry):
            here = pl.ds(pl.multiple_of(chunk * ROWS, ROWS), ROWS)
            sums = [None] * pieces
            for k in range(terms):
                before = None
                for j in range(pieces + 1):
                    block = anomaly[here, pl.ds(pl.multiple_of(starts[k] + j * LANES, LANES), LANES)]
                    rolled = pltpu.roll(block.astype(ROLL), shifts[k], 1)
                    if j:
                        weight = coef[k, :, (j - 1) * LANES : j * LANES]
                        part = jnp.concatenate(
                            [
                                jnp.where(keep[k], before[h : h + 16], rolled[h : h + 16]) * weight
                                for h in range(0, ROWS, 16)
                            ],
                            axis=0,
                        )
                        sums[j - 1] = part if k == 0 else sums[j - 1] + part
                    before = rolled
            for j in range(pieces):
                white[here, j * LANES : (j + 1) * LANES] = sums[j].astype(jnp.bfloat16)
            return carry

        lax.fori_loop(0, members // ROWS, rows, 0, unroll=2)
        acc_ref[...] += lax.dot_general(
            white[...], white[0:members, :], (((1,), (1,)), ((), ())), preferred_element_type=jnp.float32
        )


ROLL = jnp.bfloat16
ACC = jnp.bfloat16


def whiten_gram(offsets, count, predicted, left, right, observed, band):
    members, columns = predicted.shape
    terms = band.shape[0]
    tiles = columns // H
    smem = pl.BlockSpec(memory_space=pltpu.SMEM)
    enter = lambda s: (0, jnp.clip(s - 1, 0, tiles - 1))
    leave = lambda s: (0, jnp.clip(s - 2, 0, tiles - 1))
    fixed = lambda s: (0, 0)
    return pl.pallas_call(
        functools.partial(whiten_kernel, tiles),
        grid=(tiles + 2,),
        out_shape=(
            jax.ShapeDtypeStruct((members + EXTRA, members), jnp.float32),
            jax.ShapeDtypeStruct((1, columns), jnp.float32),
        ),
        in_specs=[
            smem, smem,
            pl.BlockSpec((members, H), enter),
            pl.BlockSpec((members + EXTRA, H), fixed),
            pl.BlockSpec((members + EXTRA, H), fixed),
            pl.BlockSpec((1, H), enter),
            pl.BlockSpec((terms, H), leave),
        ],
        out_specs=(
            pl.BlockSpec((members + EXTRA, members), fixed),
            pl.BlockSpec((1, H), leave),
        ),
        scratch_shapes=[
            pltpu.VMEM((members, columns + 2 * H + LANES), jnp.bfloat16),
            pltpu.VMEM((8, columns + 2 * H + LANES), jnp.float32),
            pltpu.VMEM((terms, 16, H), jnp.bfloat16),
            pltpu.VMEM((members + EXTRA, H), jnp.bfloat16),
        ],
        compiler_params=pltpu.CompilerParams(vmem_limit_bytes=48 << 20),
    )(offsets, count, predicted, left, right, observed, band)


def sum_kernel(shards, x_ref, out_ref, arrived, chunks, send_a, recv_a, send_b, recv_b):
    lines = arrived.shape[1]
    grp = lax.axis_index("grp")
    par_size = lax.axis_size("par")
    me = lax.axis_index("obs") * par_size + lax.axis_index("par")

    def where(d):
        peer = lax.rem(me + d, shards)
        return peer, (grp, peer // par_size, lax.rem(peer, par_size))

    barrier = pltpu.get_barrier_semaphore()
    for d in range(1, shards):
        pl.semaphore_signal(barrier, inc=1, device_id=where(d)[1], device_id_type=MESH)
    pl.semaphore_wait(barrier, shards - 1)
    first = []
    for d in range(1, shards):
        peer, device = where(d)
        copy = pltpu.make_async_remote_copy(
            src_ref=x_ref.at[peer], dst_ref=arrived.at[d],
            send_sem=send_a.at[d], recv_sem=recv_a.at[d], device_id=device, device_id_type=MESH,
        )
        copy.start()
        first.append(copy)
    total = x_ref[me]
    for d in range(1, shards):
        first[d - 1].wait()
        total = total + arrived[d]
    proj = total[lines - 8 : lines, :]
    chunks[...] = total[0 : lines - 8, :]
    size = lines - 8
    mine = pl.ds(pl.multiple_of(me * size, size), size)
    second = []
    for d in range(1, shards):
        peer, device = where(d)
        copy = pltpu.make_async_remote_copy(
            src_ref=chunks, dst_ref=out_ref.at[mine],
            send_sem=send_b.at[d], recv_sem=recv_b.at[d], device_id=device, device_id_type=MESH,
        )
        copy.start()
        second.append(copy)
    out_ref[mine, :] = chunks[...]
    out_ref[shards * size : shards * size + 8, :] = proj
    for d in range(1, shards):
        second[d - 1].wait()


def sum_over_shards(acc, shards):
    members = acc.shape[1]
    if shards > 1 and members % shards == 0 and (members // shards) % 8 == 0:
        size = members // shards
        chunks = acc[:members].reshape(shards, size, members)
        tail = jnp.broadcast_to(acc[members : members + 8][None], (shards, 8, members))
        vmem = pl.BlockSpec(memory_space=pltpu.VMEM)
        return pl.pallas_call(
            functools.partial(sum_kernel, shards),
            out_shape=jax.ShapeDtypeStruct((members + 8, members), jnp.float32),
            in_specs=[vmem],
            out_specs=vmem,
            scratch_shapes=[
                pltpu.VMEM((shards, size + 8, members), jnp.float32),
                pltpu.VMEM((size, members), jnp.float32),
                pltpu.SemaphoreType.DMA((shards,)),
                pltpu.SemaphoreType.DMA((shards,)),
                pltpu.SemaphoreType.DMA((shards,)),
                pltpu.SemaphoreType.DMA((shards,)),
            ],
            compiler_params=pltpu.CompilerParams(collective_id=0, has_side_effects=True),
        )(jnp.concatenate([chunks, tail], axis=1))
    return lax.psum(acc[: members + 8], ("obs", "par"))


def exact(a, b, dims):
    return lax.dot_general(
        a, b, (dims, ((), ())), precision=lax.Precision.HIGHEST, preferred_element_type=jnp.float32
    )


def transform_kernel(obs_total, x_ref, out_ref, left, right):
    members = out_ref.shape[0]
    scale = 1.0 / obs_total
    line = lax.broadcasted_iota(jnp.int32, (members, members), 0)
    column = lax.broadcasted_iota(jnp.int32, (members, members), 1)
    eye = (line == column).astype(jnp.float32)
    left[...] = x_ref[0:members, :] * scale + eye
    right[...] = eye
    small_line = lax.broadcasted_iota(jnp.int32, (BLOCK, 1), 0)
    small = (
        lax.broadcasted_iota(jnp.int32, (BLOCK, BLOCK), 0) == lax.broadcasted_iota(jnp.int32, (BLOCK, BLOCK), 1)
    ).astype(jnp.float32)
    for b in range(members // BLOCK):
        lo, hi = b * BLOCK, (b + 1) * BLOCK
        a = left[lo:hi, lo:hi]
        x = small
        for j in range(BLOCK):
            factor = a[:, j : j + 1] / a[j : j + 1, j : j + 1]
            factor = jnp.where(small_line > j, factor, 0.0)
            x = x - factor * x[j : j + 1, :]
            a = a - factor * a[j : j + 1, :]
        diagonal = jnp.sum(a * small, axis=1, keepdims=True)
        x = x * lax.rsqrt(diagonal)
        first, later = lo // LANES * LANES, hi // LANES * LANES
        top = -(-hi // LANES) * LANES
        panel_left = exact(x, left[lo:hi, first:], ((1,), (0,)))
        panel_right = exact(x, right[lo:hi, 0:top], ((1,), (0,)))
        right[lo:hi, 0:top] = panel_right
        if hi < members:
            outer = panel_left[:, later - first :]
            update_left = exact(outer, outer, ((0,), (0,)))
            update_right = exact(outer, panel_right, ((0,), (0,)))
            left[hi:, later:] = left[hi:, later:] - update_left[hi - later :, :]
            right[hi:, 0:top] = right[hi:, 0:top] - update_right[hi - later :, :]
    inverse = right[...]
    projection = (x_ref[members : members + 1, :] + x_ref[members + 1 : members + 2, :]) * (
        math.sqrt(members - 1) / obs_total
    )
    half = jnp.sum(inverse * projection, axis=1, keepdims=True)
    weights = exact(inverse, jnp.broadcast_to(half, (members, LANES)), ((0,), (0,)))[:, 0:1]
    out_ref[...] = inverse.T + weights * (1.0 / math.sqrt(members - 1))


def transform_of(total, obs_total):
    members = total.shape[1]
    return pl.pallas_call(
        functools.partial(transform_kernel, obs_total),
        out_shape=jax.ShapeDtypeStruct((members, members), jnp.float32),
        scratch_shapes=[pltpu.VMEM((members, members), jnp.float32)] * 2,
        compiler_params=pltpu.CompilerParams(vmem_limit_bytes=32 << 20),
    )(total)


def packed_edge(pred, obs):
    high = lax.reduce_precision(obs, 8, 7)
    middle = lax.reduce_precision(obs - high, 8, 7)
    low = obs - high - middle
    parts = jnp.concatenate([high, middle, low, jnp.zeros((EXTRA - 3, H), jnp.float32)], axis=0)
    return jnp.concatenate([pred, parts.astype(jnp.bfloat16)], axis=0)


def body(predicted, observed, band, offsets, rows_count, params):
    members = predicted.shape[0]
    columns = predicted.shape[1]
    axes = ("obs", "par")
    shards = lax.axis_size(axes)
    obs_total = columns * shards
    misfit_factor = math.sqrt((members - 1) / obs_total)
    up = [(i, i + 1) for i in range(shards - 1)]
    down = [(j, i) for i, j in up]
    obs_row = observed[None, :]
    left = lax.ppermute(packed_edge(predicted[:, columns - H :], obs_row[:, columns - H :]), axes, up)
    right = lax.ppermute(packed_edge(predicted[:, :H], obs_row[:, :H]), axes, down)
    acc, row = whiten_gram(
        offsets, rows_count, predicted, left, right, obs_row, band
    )
    total = sum_over_shards(acc, shards)
    transform = transform_of(total, obs_total)
    params_wide = params.astype(jnp.float32)
    param_mean = jnp.mean(params_wide, axis=1, keepdims=True)
    params_new = param_mean + jnp.dot(
        params_wide - param_mean, transform, precision=lax.Precision.HIGHEST
    )
    return (params_new, row[0] * misfit_factor)


def solution(mesh):
    in_specs = (
        P(None, ("grp", "obs", "par")),
        P(("grp", "obs", "par")),
        P(None, ("grp", "obs", "par")),
        P(),
        P(("grp", "obs", "par")),
        P(("grp", "obs", "par"), None),
    )
    out_specs = (P(("grp", "obs", "par"), None), P(("grp", "obs", "par")))
    return jax.shard_map(body, mesh=mesh, in_specs=in_specs, out_specs=out_specs, check_vma=False)
```

```python
import functools
import math

import jax
import jax.numpy as jnp
from jax import lax
from jax.experimental import pallas as pl
from jax.experimental.pallas import tpu as pltpu
from jax.sharding import PartitionSpec as P

H = 1024
LANES = 128
ROWS = 64
EXTRA = 16
BLOCK = 32
MESH = pl.DeviceIdType.MESH


def whiten_kernel(
    tiles, off_ref, count_ref, pred_ref, left_ref, right_ref, obs_ref, band_ref,
    acc_ref, misfit_ref, anomaly, innovation, coef, white,
):
    step = pl.program_id(0)
    members = pred_ref.shape[0]
    terms = band_ref.shape[0]

    def enter(pred, obs):
        wide = pred.astype(jnp.float32)
        mean = jnp.sum(wide, axis=0, keepdims=True) * (1.0 / members)
        at = pl.ds(pl.multiple_of(step * H, H), H)
        anomaly[:, at] = (wide - mean).astype(jnp.bfloat16)
        innov = (obs - mean).astype(jnp.bfloat16).astype(jnp.float32)
        innovation[:, at] = jnp.broadcast_to(innov, (8, H))

    def unpack(ref):
        parts = ref[members : members + EXTRA, :].astype(jnp.float32)
        return ref[0:members, :], parts[0:1, :] + (parts[1:2, :] + parts[2:3, :])

    @pl.when(step == 0)
    def _():
        enter(*unpack(left_ref))
        acc_ref[...] = jnp.zeros_like(acc_ref)

    @pl.when((step > 0) & (step <= tiles))
    def _():
        enter(pred_ref[...], obs_ref[...])

    @pl.when(step == tiles + 1)
    def _():
        enter(*unpack(right_ref))

    @pl.when(step >= 2)
    def _():
        tile = step - 2
        local = tile * H + lax.broadcasted_iota(jnp.int32, (1, H), 1)
        strain = ((local < count_ref[0]) | (local >= (tiles - 1) * H)).astype(jnp.float32)
        lane = lax.broadcasted_iota(jnp.int32, (16, LANES), 1)
        lane8 = lax.broadcasted_iota(jnp.int32, (8, LANES), 1)
        starts, shifts, cuts = [], [], []
        for k in range(terms):
            begin = (tile + 1) * H + off_ref[k]
            rest = lax.rem(begin, LANES)
            starts.append(begin - rest)
            shifts.append(lax.rem(LANES - rest, LANES))
            cuts.append(LANES - rest)
        pieces = H // LANES
        row_sum = [None] * pieces
        for k in range(terms):
            factor = band_ref[k : k + 1, :]
            if k:
                factor = factor * strain
            coef[k] = jnp.broadcast_to(factor.astype(jnp.bfloat16), (16, H))
            rolled = [
                pltpu.roll(
                    innovation[:, pl.ds(pl.multiple_of(starts[k] + j * LANES, LANES), LANES)], shifts[k], 1
                )
                for j in range(pieces + 1)
            ]
            for j in range(pieces):
                part = jnp.where(lane8 < cuts[k], rolled[j], rolled[j + 1])[0:1, :]
                part = part * factor[:, j * LANES : (j + 1) * LANES]
                row_sum[j] = part if k == 0 else row_sum[j] + part
        row = jnp.concatenate(row_sum, axis=1)
        misfit_ref[...] = row
        high = row.astype(jnp.bfloat16).astype(jnp.float32)
        which = lax.broadcasted_iota(jnp.int32, (EXTRA, H), 0)
        extra = jnp.where(which == 0, high, jnp.where(which == 1, row - high, 0.0))
        white[members : members + EXTRA, :] = extra.astype(jnp.bfloat16)

        keep = [lane < cut for cut in cuts]

        def rows(chunk, carry):
            here = pl.ds(pl.multiple_of(chunk * ROWS, ROWS), ROWS)
            sums = [None] * pieces
            for k in range(terms):
                before = None
                for j in range(pieces + 1):
                    block = anomaly[here, pl.ds(pl.multiple_of(starts[k] + j * LANES, LANES), LANES)]
                    rolled = pltpu.roll(block.astype(ROLL), shifts[k], 1)
                    if j:
                        weight = coef[k, :, (j - 1) * LANES : j * LANES]
                        part = jnp.concatenate(
                            [
                                jnp.where(keep[k], before[h : h + 16], rolled[h : h + 16]) * weight
                                for h in range(0, ROWS, 16)
                            ],
                            axis=0,
                        )
                        sums[j - 1] = part if k == 0 else sums[j - 1] + part
                    before = rolled
            for j in range(pieces):
                white[here, j * LANES : (j + 1) * LANES] = sums[j].astype(jnp.bfloat16)
            return carry

        lax.fori_loop(0, members // ROWS, rows, 0, unroll=4)
        acc_ref[...] += lax.dot_general(
            white[...], white[0:members, :], (((1,), (1,)), ((), ())), preferred_element_type=jnp.float32
        )


ROLL = jnp.bfloat16
ACC = jnp.bfloat16


def whiten_gram(offsets, count, predicted, left, right, observed, band):
    members, columns = predicted.shape
    terms = band.shape[0]
    tiles = columns // H
    smem = pl.BlockSpec(memory_space=pltpu.SMEM)
    enter = lambda s: (0, jnp.clip(s - 1, 0, tiles - 1))
    leave = lambda s: (0, jnp.clip(s - 2, 0, tiles - 1))
    fixed = lambda s: (0, 0)
    return pl.pallas_call(
        functools.partial(whiten_kernel, tiles),
        grid=(tiles + 2,),
        out_shape=(
            jax.ShapeDtypeStruct((members + EXTRA, members), jnp.float32),
            jax.ShapeDtypeStruct((1, columns), jnp.float32),
        ),
        in_specs=[
            smem, smem,
            pl.BlockSpec((members, H), enter),
            pl.BlockSpec((members + EXTRA, H), fixed),
            pl.BlockSpec((members + EXTRA, H), fixed),
            pl.BlockSpec((1, H), enter),
            pl.BlockSpec((terms, H), leave),
        ],
        out_specs=(
            pl.BlockSpec((members + EXTRA, members), fixed),
            pl.BlockSpec((1, H), leave),
        ),
        scratch_shapes=[
            pltpu.VMEM((members, columns + 2 * H + LANES), jnp.bfloat16),
            pltpu.VMEM((8, columns + 2 * H + LANES), jnp.float32),
            pltpu.VMEM((terms, 16, H), jnp.bfloat16),
            pltpu.VMEM((members + EXTRA, H), jnp.bfloat16),
        ],
        compiler_params=pltpu.CompilerParams(vmem_limit_bytes=48 << 20),
    )(offsets, count, predicted, left, right, observed, band)


def sum_kernel(shards, x_ref, out_ref, arrived, chunks, send_a, recv_a, send_b, recv_b):
    lines = arrived.shape[1]
    grp = lax.axis_index("grp")
    par_size = lax.axis_size("par")
    me = lax.axis_index("obs") * par_size + lax.axis_index("par")

    def where(d):
        peer = lax.rem(me + d, shards)
        return peer, (grp, peer // par_size, lax.rem(peer, par_size))

    barrier = pltpu.get_barrier_semaphore()
    for d in range(1, shards):
        pl.semaphore_signal(barrier, inc=1, device_id=where(d)[1], device_id_type=MESH)
    pl.semaphore_wait(barrier, shards - 1)
    first = []
    for d in range(1, shards):
        peer, device = where(d)
        copy = pltpu.make_async_remote_copy(
            src_ref=x_ref.at[peer], dst_ref=arrived.at[d],
            send_sem=send_a.at[d], recv_sem=recv_a.at[d], device_id=device, device_id_type=MESH,
        )
        copy.start()
        first.append(copy)
    total = x_ref[me]
    for d in range(1, shards):
        first[d - 1].wait()
        total = total + arrived[d]
    proj = total[lines - 8 : lines, :]
    chunks[...] = total[0 : lines - 8, :]
    size = lines - 8
    mine = pl.ds(pl.multiple_of(me * size, size), size)
    second = []
    for d in range(1, shards):
        peer, device = where(d)
        copy = pltpu.make_async_remote_copy(
            src_ref=chunks, dst_ref=out_ref.at[mine],
            send_sem=send_b.at[d], recv_sem=recv_b.at[d], device_id=device, device_id_type=MESH,
        )
        copy.start()
        second.append(copy)
    out_ref[mine, :] = chunks[...]
    out_ref[shards * size : shards * size + 8, :] = proj
    for d in range(1, shards):
        second[d - 1].wait()


def sum_over_shards(acc, shards):
    members = acc.shape[1]
    if shards > 1 and members % shards == 0 and (members // shards) % 8 == 0:
        size = members // shards
        chunks = acc[:members].reshape(shards, size, members)
        tail = jnp.broadcast_to(acc[members : members + 8][None], (shards, 8, members))
        vmem = pl.BlockSpec(memory_space=pltpu.VMEM)
        return pl.pallas_call(
            functools.partial(sum_kernel, shards),
            out_shape=jax.ShapeDtypeStruct((members + 8, members), jnp.float32),
            in_specs=[vmem],
            out_specs=vmem,
            scratch_shapes=[
                pltpu.VMEM((shards, size + 8, members), jnp.float32),
                pltpu.VMEM((size, members), jnp.float32),
                pltpu.SemaphoreType.DMA((shards,)),
                pltpu.SemaphoreType.DMA((shards,)),
                pltpu.SemaphoreType.DMA((shards,)),
                pltpu.SemaphoreType.DMA((shards,)),
            ],
            compiler_params=pltpu.CompilerParams(collective_id=0, has_side_effects=True),
        )(jnp.concatenate([chunks, tail], axis=1))
    return lax.psum(acc[: members + 8], ("obs", "par"))


def exact(a, b, dims):
    return lax.dot_general(
        a, b, (dims, ((), ())), precision=lax.Precision.HIGHEST, preferred_element_type=jnp.float32
    )


def transform_kernel(obs_total, x_ref, out_ref, left, right):
    members = out_ref.shape[0]
    scale = 1.0 / obs_total
    line = lax.broadcasted_iota(jnp.int32, (members, members), 0)
    column = lax.broadcasted_iota(jnp.int32, (members, members), 1)
    eye = (line == column).astype(jnp.float32)
    left[...] = x_ref[0:members, :] * scale + eye
    right[...] = eye
    small_line = lax.broadcasted_iota(jnp.int32, (BLOCK, 1), 0)
    small = (
        lax.broadcasted_iota(jnp.int32, (BLOCK, BLOCK), 0) == lax.broadcasted_iota(jnp.int32, (BLOCK, BLOCK), 1)
    ).astype(jnp.float32)
    for b in range(members // BLOCK):
        lo, hi = b * BLOCK, (b + 1) * BLOCK
        a = left[lo:hi, lo:hi]
        x = small
        for j in range(BLOCK):
            factor = a[:, j : j + 1] / a[j : j + 1, j : j + 1]
            factor = jnp.where(small_line > j, factor, 0.0)
            x = x - factor * x[j : j + 1, :]
            a = a - factor * a[j : j + 1, :]
        diagonal = jnp.sum(a * small, axis=1, keepdims=True)
        x = x * lax.rsqrt(diagonal)
        first, later = lo // LANES * LANES, hi // LANES * LANES
        top = -(-hi // LANES) * LANES
        panel_left = exact(x, left[lo:hi, first:], ((1,), (0,)))
        panel_right = exact(x, right[lo:hi, 0:top], ((1,), (0,)))
        right[lo:hi, 0:top] = panel_right
        if hi < members:
            outer = panel_left[:, later - first :]
            update_left = exact(outer, outer, ((0,), (0,)))
            update_right = exact(outer, panel_right, ((0,), (0,)))
            left[hi:, later:] = left[hi:, later:] - update_left[hi - later :, :]
            right[hi:, 0:top] = right[hi:, 0:top] - update_right[hi - later :, :]
    inverse = right[...]
    projection = (x_ref[members : members + 1, :] + x_ref[members + 1 : members + 2, :]) * (
        math.sqrt(members - 1) / obs_total
    )
    half = jnp.sum(inverse * projection, axis=1, keepdims=True)
    weights = exact(inverse, jnp.broadcast_to(half, (members, LANES)), ((0,), (0,)))[:, 0:1]
    out_ref[...] = inverse.T + weights * (1.0 / math.sqrt(members - 1))


def transform_of(total, obs_total):
    members = total.shape[1]
    return pl.pallas_call(
        functools.partial(transform_kernel, obs_total),
        out_shape=jax.ShapeDtypeStruct((members, members), jnp.float32),
        scratch_shapes=[pltpu.VMEM((members, members), jnp.float32)] * 2,
        compiler_params=pltpu.CompilerParams(vmem_limit_bytes=32 << 20),
    )(total)


def packed_edge(pred, obs):
    high = lax.reduce_precision(obs, 8, 7)
    middle = lax.reduce_precision(obs - high, 8, 7)
    low = obs - high - middle
    parts = jnp.concatenate([high, middle, low, jnp.zeros((EXTRA - 3, H), jnp.float32)], axis=0)
    return jnp.concatenate([pred, parts.astype(jnp.bfloat16)], axis=0)


def body(predicted, observed, band, offsets, rows_count, params):
    members = predicted.shape[0]
    columns = predicted.shape[1]
    axes = ("obs", "par")
    shards = lax.axis_size(axes)
    obs_total = columns * shards
    misfit_factor = math.sqrt((members - 1) / obs_total)
    up = [(i, i + 1) for i in range(shards - 1)]
    down = [(j, i) for i, j in up]
    obs_row = observed[None, :]
    left = lax.ppermute(packed_edge(predicted[:, columns - H :], obs_row[:, columns - H :]), axes, up)
    right = lax.ppermute(packed_edge(predicted[:, :H], obs_row[:, :H]), axes, down)
    acc, row = whiten_gram(
        offsets, rows_count, predicted, left, right, obs_row, band
    )
    total = sum_over_shards(acc, shards)
    transform = transform_of(total, obs_total)
    params_wide = params.astype(jnp.float32)
    param_mean = jnp.mean(params_wide, axis=1, keepdims=True)
    params_new = param_mean + jnp.dot(
        params_wide - param_mean, transform, precision=lax.Precision.HIGHEST
    )
    return (params_new, row[0] * misfit_factor)


def solution(mesh):
    in_specs = (
        P(None, ("grp", "obs", "par")),
        P(("grp", "obs", "par")),
        P(None, ("grp", "obs", "par")),
        P(),
        P(("grp", "obs", "par")),
        P(("grp", "obs", "par"), None),
    )
    out_specs = (P(("grp", "obs", "par"), None), P(("grp", "obs", "par")))
    return jax.shard_map(body, mesh=mesh, in_specs=in_specs, out_specs=out_specs, check_vma=False)
```

```python
import functools
import math

import jax
import jax.numpy as jnp
from jax import lax
from jax.experimental import pallas as pl
from jax.experimental.pallas import tpu as pltpu
from jax.sharding import PartitionSpec as P

H = 1024
LANES = 128
ROWS = 64
EXTRA = 16
BLOCK = 32
MESH = pl.DeviceIdType.MESH


def whiten_kernel(
    tiles, off_ref, count_ref, pred_ref, left_ref, right_ref, obs_ref, band_ref,
    acc_ref, misfit_ref, anomaly, innovation, coef, white,
):
    step = pl.program_id(0)
    members = pred_ref.shape[0]
    terms = band_ref.shape[0]

    def enter(pred, obs):
        wide = pred.astype(jnp.float32)
        mean = jnp.sum(wide, axis=0, keepdims=True) * (1.0 / members)
        at = pl.ds(pl.multiple_of(step * H, H), H)
        anomaly[:, at] = (wide - mean).astype(jnp.bfloat16)
        innov = (obs - mean).astype(jnp.bfloat16).astype(jnp.float32)
        innovation[:, at] = jnp.broadcast_to(innov, (8, H))

    def unpack(ref):
        parts = ref[members : members + EXTRA, :].astype(jnp.float32)
        return ref[0:members, :], parts[0:1, :] + (parts[1:2, :] + parts[2:3, :])

    @pl.when(step == 0)
    def _():
        enter(*unpack(left_ref))
        acc_ref[...] = jnp.zeros_like(acc_ref)

    @pl.when((step > 0) & (step <= tiles))
    def _():
        enter(pred_ref[...], obs_ref[...])

    @pl.when(step == tiles + 1)
    def _():
        enter(*unpack(right_ref))

    @pl.when(step >= 2)
    def _():
        tile = step - 2
        local = tile * H + lax.broadcasted_iota(jnp.int32, (1, H), 1)
        strain = ((local < count_ref[0]) | (local >= (tiles - 1) * H)).astype(jnp.float32)
        lane = lax.broadcasted_iota(jnp.int32, (16, LANES), 1)
        lane8 = lax.broadcasted_iota(jnp.int32, (8, LANES), 1)
        starts, shifts, cuts = [], [], []
        for k in range(terms):
            begin = (tile + 1) * H + off_ref[k]
            rest = lax.rem(begin, LANES)
            starts.append(begin - rest)
            shifts.append(lax.rem(LANES - rest, LANES))
            cuts.append(LANES - rest)
        pieces = H // LANES
        row_sum = [None] * pieces
        for k in range(terms):
            factor = band_ref[k : k + 1, :]
            if k:
                factor = factor * strain
            coef[k] = jnp.broadcast_to(factor.astype(jnp.bfloat16), (16, H))
            rolled = [
                pltpu.roll(
                    innovation[:, pl.ds(pl.multiple_of(starts[k] + j * LANES, LANES), LANES)], shifts[k], 1
                )
                for j in range(pieces + 1)
            ]
            for j in range(pieces):
                part = jnp.where(lane8 < cuts[k], rolled[j], rolled[j + 1])[0:1, :]
                part = part * factor[:, j * LANES : (j + 1) * LANES]
                row_sum[j] = part if k == 0 else row_sum[j] + part
        row = jnp.concatenate(row_sum, axis=1)
        misfit_ref[...] = row
        high = row.astype(jnp.bfloat16).astype(jnp.float32)
        which = lax.broadcasted_iota(jnp.int32, (EXTRA, H), 0)
        extra = jnp.where(which == 0, high, jnp.where(which == 1, row - high, 0.0))
        white[members : members + EXTRA, :] = extra.astype(jnp.bfloat16)

        keep = [lane < cut for cut in cuts]

        def rows(chunk, carry):
            here = pl.ds(pl.multiple_of(chunk * ROWS, ROWS), ROWS)
            sums = [None] * pieces
            for k in range(terms):
                before = None
                for j in range(pieces + 1):
                    block = anomaly[here, pl.ds(pl.multiple_of(starts[k] + j * LANES, LANES), LANES)]
                    rolled = pltpu.roll(block.astype(ROLL), shifts[k], 1)
                    if j:
                        weight = coef[k, :, (j - 1) * LANES : j * LANES]
                        part = jnp.concatenate(
                            [
                                jnp.where(keep[k], before[h : h + 16], rolled[h : h + 16]) * weight
                                for h in range(0, ROWS, 16)
                            ],
                            axis=0,
                        )
                        sums[j - 1] = part if k == 0 else sums[j - 1] + part
                    before = rolled
            for j in range(pieces):
                white[here, j * LANES : (j + 1) * LANES] = sums[j].astype(jnp.bfloat16)
            return carry

        lax.fori_loop(0, members // ROWS, rows, 0, unroll=4)
        acc_ref[...] += lax.dot_general(
            white[...], white[0:members, :], (((1,), (1,)), ((), ())), preferred_element_type=jnp.float32
        )


ROLL = jnp.bfloat16
ACC = jnp.bfloat16


def whiten_gram(offsets, count, predicted, left, right, observed, band):
    members, columns = predicted.shape
    terms = band.shape[0]
    tiles = columns // H
    smem = pl.BlockSpec(memory_space=pltpu.SMEM)
    enter = lambda s: (0, jnp.clip(s - 1, 0, tiles - 1))
    leave = lambda s: (0, jnp.clip(s - 2, 0, tiles - 1))
    fixed = lambda s: (0, 0)
    return pl.pallas_call(
        functools.partial(whiten_kernel, tiles),
        grid=(tiles + 2,),
        out_shape=(
            jax.ShapeDtypeStruct((members + EXTRA, members), jnp.float32),
            jax.ShapeDtypeStruct((1, columns), jnp.float32),
        ),
        in_specs=[
            smem, smem,
            pl.BlockSpec((members, H), enter),
            pl.BlockSpec((members + EXTRA, H), fixed),
            pl.BlockSpec((members + EXTRA, H), fixed),
            pl.BlockSpec((1, H), enter),
            pl.BlockSpec((terms, H), leave),
        ],
        out_specs=(
            pl.BlockSpec((members + EXTRA, members), fixed),
            pl.BlockSpec((1, H), leave),
        ),
        scratch_shapes=[
            pltpu.VMEM((members, columns + 2 * H + LANES), jnp.bfloat16),
            pltpu.VMEM((8, columns + 2 * H + LANES), jnp.float32),
            pltpu.VMEM((terms, 16, H), jnp.bfloat16),
            pltpu.VMEM((members + EXTRA, H), jnp.bfloat16),
        ],
        compiler_params=pltpu.CompilerParams(vmem_limit_bytes=62 << 20),
    )(offsets, count, predicted, left, right, observed, band)


def sum_kernel(shards, x_ref, out_ref, arrived, chunks, send_a, recv_a, send_b, recv_b):
    lines = arrived.shape[1]
    grp = lax.axis_index("grp")
    par_size = lax.axis_size("par")
    me = lax.axis_index("obs") * par_size + lax.axis_index("par")

    def where(d):
        peer = lax.rem(me + d, shards)
        return peer, (grp, peer // par_size, lax.rem(peer, par_size))

    barrier = pltpu.get_barrier_semaphore()
    for d in range(1, shards):
        pl.semaphore_signal(barrier, inc=1, device_id=where(d)[1], device_id_type=MESH)
    pl.semaphore_wait(barrier, shards - 1)
    first = []
    for d in range(1, shards):
        peer, device = where(d)
        copy = pltpu.make_async_remote_copy(
            src_ref=x_ref.at[peer], dst_ref=arrived.at[d],
            send_sem=send_a.at[d], recv_sem=recv_a.at[d], device_id=device, device_id_type=MESH,
        )
        copy.start()
        first.append(copy)
    total = x_ref[me]
    for d in range(1, shards):
        first[d - 1].wait()
        total = total + arrived[d]
    proj = total[lines - 8 : lines, :]
    chunks[...] = total[0 : lines - 8, :]
    size = lines - 8
    mine = pl.ds(pl.multiple_of(me * size, size), size)
    second = []
    for d in range(1, shards):
        peer, device = where(d)
        copy = pltpu.make_async_remote_copy(
            src_ref=chunks, dst_ref=out_ref.at[mine],
            send_sem=send_b.at[d], recv_sem=recv_b.at[d], device_id=device, device_id_type=MESH,
        )
        copy.start()
        second.append(copy)
    out_ref[mine, :] = chunks[...]
    out_ref[shards * size : shards * size + 8, :] = proj
    for d in range(1, shards):
        second[d - 1].wait()


def sum_over_shards(acc, shards):
    members = acc.shape[1]
    if shards > 1 and members % shards == 0 and (members // shards) % 8 == 0:
        size = members // shards
        chunks = acc[:members].reshape(shards, size, members)
        tail = jnp.broadcast_to(acc[members : members + 8][None], (shards, 8, members))
        vmem = pl.BlockSpec(memory_space=pltpu.VMEM)
        return pl.pallas_call(
            functools.partial(sum_kernel, shards),
            out_shape=jax.ShapeDtypeStruct((members + 8, members), jnp.float32),
            in_specs=[vmem],
            out_specs=vmem,
            scratch_shapes=[
                pltpu.VMEM((shards, size + 8, members), jnp.float32),
                pltpu.VMEM((size, members), jnp.float32),
                pltpu.SemaphoreType.DMA((shards,)),
                pltpu.SemaphoreType.DMA((shards,)),
                pltpu.SemaphoreType.DMA((shards,)),
                pltpu.SemaphoreType.DMA((shards,)),
            ],
            compiler_params=pltpu.CompilerParams(collective_id=0, has_side_effects=True),
        )(jnp.concatenate([chunks, tail], axis=1))
    return lax.psum(acc[: members + 8], ("obs", "par"))


def exact(a, b, dims):
    return lax.dot_general(
        a, b, (dims, ((), ())), precision=lax.Precision.HIGHEST, preferred_element_type=jnp.float32
    )


def transform_kernel(obs_total, x_ref, out_ref, left, right):
    members = out_ref.shape[0]
    scale = 1.0 / obs_total
    line = lax.broadcasted_iota(jnp.int32, (members, members), 0)
    column = lax.broadcasted_iota(jnp.int32, (members, members), 1)
    eye = (line == column).astype(jnp.float32)
    left[...] = x_ref[0:members, :] * scale + eye
    right[...] = eye
    small_line = lax.broadcasted_iota(jnp.int32, (BLOCK, 1), 0)
    small = (
        lax.broadcasted_iota(jnp.int32, (BLOCK, BLOCK), 0) == lax.broadcasted_iota(jnp.int32, (BLOCK, BLOCK), 1)
    ).astype(jnp.float32)
    for b in range(members // BLOCK):
        lo, hi = b * BLOCK, (b + 1) * BLOCK
        a = left[lo:hi, lo:hi]
        x = small
        for j in range(BLOCK):
            factor = a[:, j : j + 1] / a[j : j + 1, j : j + 1]
            factor = jnp.where(small_line > j, factor, 0.0)
            x = x - factor * x[j : j + 1, :]
            a = a - factor * a[j : j + 1, :]
        diagonal = jnp.sum(a * small, axis=1, keepdims=True)
        x = x * lax.rsqrt(diagonal)
        first, later = lo // LANES * LANES, hi // LANES * LANES
        top = -(-hi // LANES) * LANES
        panel_left = exact(x, left[lo:hi, first:], ((1,), (0,)))
        panel_right = exact(x, right[lo:hi, 0:top], ((1,), (0,)))
        right[lo:hi, 0:top] = panel_right
        if hi < members:
            outer = panel_left[:, later - first :]
            update_left = exact(outer, outer, ((0,), (0,)))
            update_right = exact(outer, panel_right, ((0,), (0,)))
            left[hi:, later:] = left[hi:, later:] - update_left[hi - later :, :]
            right[hi:, 0:top] = right[hi:, 0:top] - update_right[hi - later :, :]
    inverse = right[...]
    projection = (x_ref[members : members + 1, :] + x_ref[members + 1 : members + 2, :]) * (
        math.sqrt(members - 1) / obs_total
    )
    half = jnp.sum(inverse * projection, axis=1, keepdims=True)
    weights = exact(inverse, jnp.broadcast_to(half, (members, LANES)), ((0,), (0,)))[:, 0:1]
    out_ref[...] = inverse.T + weights * (1.0 / math.sqrt(members - 1))


def transform_of(total, obs_total):
    members = total.shape[1]
    return pl.pallas_call(
        functools.partial(transform_kernel, obs_total),
        out_shape=jax.ShapeDtypeStruct((members, members), jnp.float32),
        scratch_shapes=[pltpu.VMEM((members, members), jnp.float32)] * 2,
        compiler_params=pltpu.CompilerParams(vmem_limit_bytes=32 << 20),
    )(total)


def packed_edge(pred, obs):
    high = lax.reduce_precision(obs, 8, 7)
    middle = lax.reduce_precision(obs - high, 8, 7)
    low = obs - high - middle
    parts = jnp.concatenate([high, middle, low, jnp.zeros((EXTRA - 3, H), jnp.float32)], axis=0)
    return jnp.concatenate([pred, parts.astype(jnp.bfloat16)], axis=0)


def body(predicted, observed, band, offsets, rows_count, params):
    members = predicted.shape[0]
    columns = predicted.shape[1]
    axes = ("obs", "par")
    shards = lax.axis_size(axes)
    obs_total = columns * shards
    misfit_factor = math.sqrt((members - 1) / obs_total)
    up = [(i, i + 1) for i in range(shards - 1)]
    down = [(j, i) for i, j in up]
    obs_row = observed[None, :]
    left = lax.ppermute(packed_edge(predicted[:, columns - H :], obs_row[:, columns - H :]), axes, up)
    right = lax.ppermute(packed_edge(predicted[:, :H], obs_row[:, :H]), axes, down)
    acc, row = whiten_gram(
        offsets, rows_count, predicted, left, right, obs_row, band
    )
    total = sum_over_shards(acc, shards)
    transform = transform_of(total, obs_total)
    params_wide = params.astype(jnp.float32)
    param_mean = jnp.mean(params_wide, axis=1, keepdims=True)
    params_new = param_mean + jnp.dot(
        params_wide - param_mean, transform, precision=lax.Precision.HIGHEST
    )
    return (params_new, row[0] * misfit_factor)


def solution(mesh):
    in_specs = (
        P(None, ("grp", "obs", "par")),
        P(("grp", "obs", "par")),
        P(None, ("grp", "obs", "par")),
        P(),
        P(("grp", "obs", "par")),
        P(("grp", "obs", "par"), None),
    )
    out_specs = (P(("grp", "obs", "par"), None), P(("grp", "obs", "par")))
    return jax.shard_map(body, mesh=mesh, in_specs=in_specs, out_specs=out_specs, check_vma=False)
```

```python
import functools
import math

import jax
import jax.numpy as jnp
from jax import lax
from jax.experimental import pallas as pl
from jax.experimental.pallas import tpu as pltpu
from jax.sharding import PartitionSpec as P

H = 1024
LANES = 128
ROWS = 64
EXTRA = 16
BLOCK = 32
MESH = pl.DeviceIdType.MESH


def whiten_kernel(
    tiles, off_ref, count_ref, pred_ref, left_ref, right_ref, obs_ref, band_ref,
    acc_ref, misfit_ref, anomaly, innovation, coef, white,
):
    step = pl.program_id(0)
    members = pred_ref.shape[0]
    terms = band_ref.shape[0]

    def enter(pred, obs):
        wide = pred.astype(jnp.float32)
        mean = jnp.sum(wide, axis=0, keepdims=True) * (1.0 / members)
        at = pl.ds(pl.multiple_of(step * H, H), H)
        anomaly[:, at] = (wide - mean).astype(jnp.bfloat16)
        innov = (obs - mean).astype(jnp.bfloat16).astype(jnp.float32)
        innovation[:, at] = jnp.broadcast_to(innov, (8, H))

    def unpack(ref):
        parts = ref[members : members + EXTRA, :].astype(jnp.float32)
        return ref[0:members, :], parts[0:1, :] + (parts[1:2, :] + parts[2:3, :])

    @pl.when(step == 0)
    def _():
        enter(*unpack(left_ref))
        acc_ref[...] = jnp.zeros_like(acc_ref)

    @pl.when((step > 0) & (step <= tiles))
    def _():
        enter(pred_ref[...], obs_ref[...])

    @pl.when(step == tiles + 1)
    def _():
        enter(*unpack(right_ref))

    @pl.when(step >= 2)
    def _():
        tile = step - 2
        local = tile * H + lax.broadcasted_iota(jnp.int32, (1, H), 1)
        strain = ((local < count_ref[0]) | (local >= (tiles - 1) * H)).astype(jnp.float32)
        lane = lax.broadcasted_iota(jnp.int32, (16, LANES), 1)
        lane8 = lax.broadcasted_iota(jnp.int32, (8, LANES), 1)
        starts, shifts, cuts = [], [], []
        for k in range(terms):
            begin = (tile + 1) * H + off_ref[k]
            rest = lax.rem(begin, LANES)
            starts.append(begin - rest)
            shifts.append(lax.rem(LANES - rest, LANES))
            cuts.append(LANES - rest)
        pieces = H // LANES
        row_sum = [None] * pieces
        for k in range(terms):
            factor = band_ref[k : k + 1, :]
            if k:
                factor = factor * strain
            coef[k] = jnp.broadcast_to(factor.astype(jnp.bfloat16), (16, H))
            rolled = [
                pltpu.roll(
                    innovation[:, pl.ds(pl.multiple_of(starts[k] + j * LANES, LANES), LANES)], shifts[k], 1
                )
                for j in range(pieces + 1)
            ]
            for j in range(pieces):
                part = jnp.where(lane8 < cuts[k], rolled[j], rolled[j + 1])[0:1, :]
                part = part * factor[:, j * LANES : (j + 1) * LANES]
                row_sum[j] = part if k == 0 else row_sum[j] + part
        row = jnp.concatenate(row_sum, axis=1)
        misfit_ref[...] = row
        high = row.astype(jnp.bfloat16).astype(jnp.float32)
        which = lax.broadcasted_iota(jnp.int32, (EXTRA, H), 0)
        extra = jnp.where(which == 0, high, jnp.where(which == 1, row - high, 0.0))
        white[members : members + EXTRA, :] = extra.astype(jnp.bfloat16)

        keep = [lane < cut for cut in cuts]

        def rows(chunk, carry):
            here = pl.ds(pl.multiple_of(chunk * ROWS, ROWS), ROWS)
            sums = [None] * pieces
            for k in range(terms):
                before = None
                for j in range(pieces + 1):
                    block = anomaly[here, pl.ds(pl.multiple_of(starts[k] + j * LANES, LANES), LANES)]
                    rolled = pltpu.roll(block.astype(ROLL), shifts[k], 1)
                    if j:
                        weight = coef[k, :, (j - 1) * LANES : j * LANES]
                        part = jnp.concatenate(
                            [
                                jnp.where(keep[k], before[h : h + 16], rolled[h : h + 16]) * weight
                                for h in range(0, ROWS, 16)
                            ],
                            axis=0,
                        )
                        sums[j - 1] = part if k == 0 else sums[j - 1] + part
                    before = rolled
            for j in range(pieces):
                white[here, j * LANES : (j + 1) * LANES] = sums[j].astype(jnp.bfloat16)
            return carry

        lax.fori_loop(0, members // ROWS, rows, 0, unroll=4)
        acc_ref[...] += lax.dot_general(
            white[...], white[0:members, :], (((1,), (1,)), ((), ())), preferred_element_type=jnp.float32
        )


ROLL = jnp.bfloat16
ACC = jnp.bfloat16


def whiten_gram(offsets, count, predicted, left, right, observed, band):
    members, columns = predicted.shape
    terms = band.shape[0]
    tiles = columns // H
    smem = pl.BlockSpec(memory_space=pltpu.SMEM)
    enter = lambda s: (0, jnp.clip(s - 1, 0, tiles - 1))
    leave = lambda s: (0, jnp.clip(s - 2, 0, tiles - 1))
    fixed = lambda s: (0, 0)
    return pl.pallas_call(
        functools.partial(whiten_kernel, tiles),
        grid=(tiles + 2,),
        out_shape=(
            jax.ShapeDtypeStruct((members + EXTRA, members), jnp.float32),
            jax.ShapeDtypeStruct((1, columns), jnp.float32),
        ),
        in_specs=[
            smem, smem,
            pl.BlockSpec((members, H), enter),
            pl.BlockSpec((members + EXTRA, H), fixed),
            pl.BlockSpec((members + EXTRA, H), fixed),
            pl.BlockSpec((1, H), enter),
            pl.BlockSpec((terms, H), leave),
        ],
        out_specs=(
            pl.BlockSpec((members + EXTRA, members), fixed),
            pl.BlockSpec((1, H), leave),
        ),
        scratch_shapes=[
            pltpu.VMEM((members, columns + 2 * H + LANES), jnp.bfloat16),
            pltpu.VMEM((8, columns + 2 * H + LANES), jnp.float32),
            pltpu.VMEM((terms, 16, H), jnp.bfloat16),
            pltpu.VMEM((members + EXTRA, H), jnp.bfloat16),
        ],
        compiler_params=pltpu.CompilerParams(vmem_limit_bytes=48 << 20),
    )(offsets, count, predicted, left, right, observed, band)


def sum_kernel(shards, x_ref, out_ref, arrived, chunks, send_a, recv_a, send_b, recv_b):
    grp = lax.axis_index("grp")
    par_size = lax.axis_size("par")
    me = lax.axis_index("obs") * par_size + lax.axis_index("par")

    def where(d):
        peer = lax.rem(me + d, shards)
        return peer, (grp, peer // par_size, lax.rem(peer, par_size))

    barrier = pltpu.get_barrier_semaphore()
    for d in range(1, shards):
        pl.semaphore_signal(barrier, inc=1, device_id=where(d)[1], device_id_type=MESH)
    pl.semaphore_wait(barrier, shards - 1)
    first = []
    for d in range(1, shards):
        peer, device = where(d)
        copy = pltpu.make_async_remote_copy(
            src_ref=x_ref.at[peer], dst_ref=arrived.at[d],
            send_sem=send_a.at[d], recv_sem=recv_a.at[d], device_id=device, device_id_type=MESH,
        )
        copy.start()
        first.append(copy)
    total = x_ref[me]
    for d in range(1, shards):
        first[d - 1].wait()
        total = total + arrived[d]
    chunks[...] = total
    second = []
    for d in range(1, shards):
        peer, device = where(d)
        copy = pltpu.make_async_remote_copy(
            src_ref=chunks, dst_ref=out_ref.at[me],
            send_sem=send_b.at[d], recv_sem=recv_b.at[d], device_id=device, device_id_type=MESH,
        )
        copy.start()
        second.append(copy)
    out_ref[me] = total
    for d in range(1, shards):
        second[d - 1].wait()


def sum_over_shards(acc, shards):
    members = acc.shape[1]
    half = members // 2
    direct = shards > 1 and 3 * half % (8 * shards) == 0
    parts = shards if direct else 2
    size = 3 * half // parts
    gram = jnp.concatenate([acc[:members, :half], acc[half:members, half:]], axis=0).reshape(parts, size, half)
    proj = (acc[members] + acc[members + 1]).reshape(2, 1, half)
    tail = jnp.concatenate([proj, jnp.zeros((parts - 2, 1, half), jnp.float32)], axis=0) if parts > 2 else proj
    packed = jnp.concatenate([gram, tail], axis=1)
    if not direct:
        return lax.psum(packed, ("obs", "par"))
    vmem = pl.BlockSpec(memory_space=pltpu.VMEM)
    return pl.pallas_call(
        functools.partial(sum_kernel, shards),
        out_shape=jax.ShapeDtypeStruct(packed.shape, jnp.float32),
        in_specs=[vmem],
        out_specs=vmem,
        scratch_shapes=[
            pltpu.VMEM(packed.shape, jnp.float32),
            pltpu.VMEM(packed.shape[1:], jnp.float32),
            pltpu.SemaphoreType.DMA((shards,)),
            pltpu.SemaphoreType.DMA((shards,)),
            pltpu.SemaphoreType.DMA((shards,)),
            pltpu.SemaphoreType.DMA((shards,)),
        ],
        compiler_params=pltpu.CompilerParams(collective_id=0, has_side_effects=True),
    )(packed)


def exact(a, b, dims):
    return lax.dot_general(
        a, b, (dims, ((), ())), precision=lax.Precision.HIGHEST, preferred_element_type=jnp.float32
    )


def transform_kernel(obs_total, x_ref, out_ref, left, right):
    members = out_ref.shape[0]
    scale = 1.0 / obs_total
    line = lax.broadcasted_iota(jnp.int32, (members, members), 0)
    column = lax.broadcasted_iota(jnp.int32, (members, members), 1)
    eye = (line == column).astype(jnp.float32)
    half = members // 2
    parts = x_ref.shape[0]
    size = x_ref.shape[1] - 1
    stacked = jnp.concatenate([x_ref[d, 0:size, :] for d in range(parts)], axis=0)
    gram = jnp.concatenate(
        [
            jnp.concatenate([stacked[0:half], stacked[half:members].T], axis=1),
            jnp.concatenate([stacked[half:members], stacked[members:]], axis=1),
        ],
        axis=0,
    )
    left[...] = gram * scale + eye
    right[...] = eye
    small_line = lax.broadcasted_iota(jnp.int32, (BLOCK, 1), 0)
    small = (
        lax.broadcasted_iota(jnp.int32, (BLOCK, BLOCK), 0) == lax.broadcasted_iota(jnp.int32, (BLOCK, BLOCK), 1)
    ).astype(jnp.float32)
    for b in range(members // BLOCK):
        lo, hi = b * BLOCK, (b + 1) * BLOCK
        a = left[lo:hi, lo:hi]
        x = small
        for j in range(BLOCK):
            factor = a[:, j : j + 1] / a[j : j + 1, j : j + 1]
            factor = jnp.where(small_line > j, factor, 0.0)
            x = x - factor * x[j : j + 1, :]
            a = a - factor * a[j : j + 1, :]
        diagonal = jnp.sum(a * small, axis=1, keepdims=True)
        x = x * lax.rsqrt(diagonal)
        first, later = lo // LANES * LANES, hi // LANES * LANES
        top = -(-hi // LANES) * LANES
        panel_left = exact(x, left[lo:hi, first:], ((1,), (0,)))
        panel_right = exact(x, right[lo:hi, 0:top], ((1,), (0,)))
        right[lo:hi, 0:top] = panel_right
        if hi < members:
            outer = panel_left[:, later - first :]
            update_left = exact(outer, outer, ((0,), (0,)))
            update_right = exact(outer, panel_right, ((0,), (0,)))
            left[hi:, later:] = left[hi:, later:] - update_left[hi - later :, :]
            right[hi:, 0:top] = right[hi:, 0:top] - update_right[hi - later :, :]
    inverse = right[...]
    projection = jnp.concatenate([x_ref[0, size : size + 1, :], x_ref[1, size : size + 1, :]], axis=1) * (
        math.sqrt(members - 1) / obs_total
    )
    half = jnp.sum(inverse * projection, axis=1, keepdims=True)
    weights = exact(inverse, jnp.broadcast_to(half, (members, LANES)), ((0,), (0,)))[:, 0:1]
    out_ref[...] = inverse.T + weights * (1.0 / math.sqrt(members - 1))


def transform_of(total, obs_total):
    members = 2 * total.shape[2]
    return pl.pallas_call(
        functools.partial(transform_kernel, obs_total),
        out_shape=jax.ShapeDtypeStruct((members, members), jnp.float32),
        scratch_shapes=[pltpu.VMEM((members, members), jnp.float32)] * 2,
        compiler_params=pltpu.CompilerParams(vmem_limit_bytes=32 << 20),
    )(total)


def packed_edge(pred, obs):
    high = lax.reduce_precision(obs, 8, 7)
    middle = lax.reduce_precision(obs - high, 8, 7)
    low = obs - high - middle
    parts = jnp.concatenate([high, middle, low, jnp.zeros((EXTRA - 3, H), jnp.float32)], axis=0)
    return jnp.concatenate([pred, parts.astype(jnp.bfloat16)], axis=0)


def body(predicted, observed, band, offsets, rows_count, params):
    members = predicted.shape[0]
    columns = predicted.shape[1]
    axes = ("obs", "par")
    shards = lax.axis_size(axes)
    obs_total = columns * shards
    misfit_factor = math.sqrt((members - 1) / obs_total)
    up = [(i, i + 1) for i in range(shards - 1)]
    down = [(j, i) for i, j in up]
    obs_row = observed[None, :]
    left = lax.ppermute(packed_edge(predicted[:, columns - H :], obs_row[:, columns - H :]), axes, up)
    right = lax.ppermute(packed_edge(predicted[:, :H], obs_row[:, :H]), axes, down)
    acc, row = whiten_gram(
        offsets, rows_count, predicted, left, right, obs_row, band
    )
    total = sum_over_shards(acc, shards)
    transform = transform_of(total, obs_total)
    params_wide = params.astype(jnp.float32)
    param_mean = jnp.mean(params_wide, axis=1, keepdims=True)
    params_new = param_mean + jnp.dot(
        params_wide - param_mean, transform, precision=lax.Precision.HIGHEST
    )
    return (params_new, row[0] * misfit_factor)


def solution(mesh):
    in_specs = (
        P(None, ("grp", "obs", "par")),
        P(("grp", "obs", "par")),
        P(None, ("grp", "obs", "par")),
        P(),
        P(("grp", "obs", "par")),
        P(("grp", "obs", "par"), None),
    )
    out_specs = (P(("grp", "obs", "par"), None), P(("grp", "obs", "par")))
    return jax.shard_map(body, mesh=mesh, in_specs=in_specs, out_specs=out_specs, check_vma=False)
```

```python
import functools
import math

import jax
import jax.numpy as jnp
from jax import lax
from jax.experimental import pallas as pl
from jax.experimental.pallas import tpu as pltpu
from jax.sharding import PartitionSpec as P

H = 1024
LANES = 128
ROWS = 64
EXTRA = 16
BLOCK = 32
MESH = pl.DeviceIdType.MESH


def whiten_kernel(
    tiles, off_ref, count_ref, pred_ref, left_ref, right_ref, obs_ref, band_ref,
    acc_ref, misfit_ref, anomaly, innovation, coef, white,
):
    step = pl.program_id(0)
    members = pred_ref.shape[0]
    terms = band_ref.shape[0]

    def enter(pred, obs):
        wide = pred.astype(jnp.float32)
        mean = jnp.sum(wide, axis=0, keepdims=True) * (1.0 / members)
        at = pl.ds(pl.multiple_of(step * H, H), H)
        anomaly[:, at] = (wide - mean).astype(jnp.bfloat16)
        innov = (obs - mean).astype(jnp.bfloat16).astype(jnp.float32)
        innovation[:, at] = jnp.broadcast_to(innov, (8, H))

    def unpack(ref):
        parts = ref[members : members + EXTRA, :].astype(jnp.float32)
        return ref[0:members, :], parts[0:1, :] + (parts[1:2, :] + parts[2:3, :])

    @pl.when(step == 0)
    def _():
        enter(*unpack(left_ref))
        acc_ref[...] = jnp.zeros_like(acc_ref)

    @pl.when((step > 0) & (step <= tiles))
    def _():
        enter(pred_ref[...], obs_ref[...])

    @pl.when(step == tiles + 1)
    def _():
        enter(*unpack(right_ref))

    @pl.when(step >= 2)
    def _():
        tile = step - 2
        local = tile * H + lax.broadcasted_iota(jnp.int32, (1, H), 1)
        strain = ((local < count_ref[0]) | (local >= (tiles - 1) * H)).astype(jnp.float32)
        lane = lax.broadcasted_iota(jnp.int32, (16, LANES), 1)
        lane8 = lax.broadcasted_iota(jnp.int32, (8, LANES), 1)
        starts, shifts, cuts = [], [], []
        for k in range(terms):
            begin = (tile + 1) * H + off_ref[k]
            rest = lax.rem(begin, LANES)
            starts.append(begin - rest)
            shifts.append(lax.rem(LANES - rest, LANES))
            cuts.append(LANES - rest)
        pieces = H // LANES
        row_sum = [None] * pieces
        for k in range(terms):
            factor = band_ref[k : k + 1, :]
            if k:
                factor = factor * strain
            coef[k] = jnp.broadcast_to(factor.astype(jnp.bfloat16), (16, H))
            rolled = [
                pltpu.roll(
                    innovation[:, pl.ds(pl.multiple_of(starts[k] + j * LANES, LANES), LANES)], shifts[k], 1
                )
                for j in range(pieces + 1)
            ]
            for j in range(pieces):
                part = jnp.where(lane8 < cuts[k], rolled[j], rolled[j + 1])[0:1, :]
                part = part * factor[:, j * LANES : (j + 1) * LANES]
                row_sum[j] = part if k == 0 else row_sum[j] + part
        row = jnp.concatenate(row_sum, axis=1)
        misfit_ref[...] = row
        high = row.astype(jnp.bfloat16).astype(jnp.float32)
        which = lax.broadcasted_iota(jnp.int32, (EXTRA, H), 0)
        extra = jnp.where(which == 0, high, jnp.where(which == 1, row - high, 0.0))
        white[members : members + EXTRA, :] = extra.astype(jnp.bfloat16)

        keep = [lane < cut for cut in cuts]

        def rows(chunk, carry):
            here = pl.ds(pl.multiple_of(chunk * ROWS, ROWS), ROWS)
            sums = [None] * pieces
            for k in range(terms):
                before = None
                for j in range(pieces + 1):
                    block = anomaly[here, pl.ds(pl.multiple_of(starts[k] + j * LANES, LANES), LANES)]
                    rolled = pltpu.roll(block.astype(ROLL), shifts[k], 1)
                    if j:
                        weight = coef[k, :, (j - 1) * LANES : j * LANES]
                        part = jnp.concatenate(
                            [
                                jnp.where(keep[k], before[h : h + 16], rolled[h : h + 16]) * weight
                                for h in range(0, ROWS, 16)
                            ],
                            axis=0,
                        )
                        sums[j - 1] = part if k == 0 else sums[j - 1] + part
                    before = rolled
            for j in range(pieces):
                white[here, j * LANES : (j + 1) * LANES] = sums[j].astype(jnp.bfloat16)
            return carry

        lax.fori_loop(0, members // ROWS, rows, 0, unroll=4)
        acc_ref[...] += lax.dot_general(
            white[...], white[0:members, :], (((1,), (1,)), ((), ())), preferred_element_type=jnp.float32
        )


ROLL = jnp.bfloat16
ACC = jnp.bfloat16


def whiten_gram(offsets, count, predicted, left, right, observed, band):
    members, columns = predicted.shape
    terms = band.shape[0]
    tiles = columns // H
    smem = pl.BlockSpec(memory_space=pltpu.SMEM)
    enter = lambda s: (0, jnp.clip(s - 1, 0, tiles - 1))
    leave = lambda s: (0, jnp.clip(s - 2, 0, tiles - 1))
    fixed = lambda s: (0, 0)
    return pl.pallas_call(
        functools.partial(whiten_kernel, tiles),
        grid=(tiles + 2,),
        out_shape=(
            jax.ShapeDtypeStruct((members + EXTRA, members), jnp.float32),
            jax.ShapeDtypeStruct((1, columns), jnp.float32),
        ),
        in_specs=[
            smem, smem,
            pl.BlockSpec((members, H), enter),
            pl.BlockSpec((members + EXTRA, H), fixed),
            pl.BlockSpec((members + EXTRA, H), fixed),
            pl.BlockSpec((1, H), enter),
            pl.BlockSpec((terms, H), leave),
        ],
        out_specs=(
            pl.BlockSpec((members + EXTRA, members), fixed),
            pl.BlockSpec((1, H), leave),
        ),
        scratch_shapes=[
            pltpu.VMEM((members, columns + 2 * H + LANES), jnp.bfloat16),
            pltpu.VMEM((8, columns + 2 * H + LANES), jnp.float32),
            pltpu.VMEM((terms, 16, H), jnp.bfloat16),
            pltpu.VMEM((members + EXTRA, H), jnp.bfloat16),
        ],
        compiler_params=pltpu.CompilerParams(vmem_limit_bytes=48 << 20),
    )(offsets, count, predicted, left, right, observed, band)


def sum_kernel(shards, x_ref, out_ref, arrived, chunks, send_a, recv_a, send_b, recv_b):
    grp = lax.axis_index("grp")
    par_size = lax.axis_size("par")
    me = lax.axis_index("obs") * par_size + lax.axis_index("par")

    def where(d):
        peer = lax.rem(me + d, shards)
        return peer, (grp, peer // par_size, lax.rem(peer, par_size))

    barrier = pltpu.get_barrier_semaphore()
    for d in range(1, shards):
        pl.semaphore_signal(barrier, inc=1, device_id=where(d)[1], device_id_type=MESH)
    pl.semaphore_wait(barrier, shards - 1)
    order = sorted(range(1, shards), key=lambda d: -min(d, shards - d))
    first = []
    for d in order:
        peer, device = where(d)
        copy = pltpu.make_async_remote_copy(
            src_ref=x_ref.at[peer], dst_ref=arrived.at[d],
            send_sem=send_a.at[d], recv_sem=recv_a.at[d], device_id=device, device_id_type=MESH,
        )
        copy.start()
        first.append(copy)
    total = x_ref[me]
    for d in order:
        first[order.index(d)].wait()
        total = total + arrived[d]
    chunks[...] = total
    second = []
    for d in order:
        peer, device = where(d)
        copy = pltpu.make_async_remote_copy(
            src_ref=chunks, dst_ref=out_ref.at[me],
            send_sem=send_b.at[d], recv_sem=recv_b.at[d], device_id=device, device_id_type=MESH,
        )
        copy.start()
        second.append(copy)
    out_ref[me] = total
    for d in order:
        second[order.index(d)].wait()


def sum_over_shards(acc, shards):
    members = acc.shape[1]
    half = members // 2
    direct = shards > 1 and 3 * half % (8 * shards) == 0
    parts = shards if direct else 2
    size = 3 * half // parts
    gram = jnp.concatenate([acc[:members, :half], acc[half:members, half:]], axis=0).reshape(parts, size, half)
    proj = (acc[members] + acc[members + 1]).reshape(2, 1, half)
    tail = jnp.concatenate([proj, jnp.zeros((parts - 2, 1, half), jnp.float32)], axis=0) if parts > 2 else proj
    packed = jnp.concatenate([gram, tail], axis=1)
    if not direct:
        return lax.psum(packed, ("obs", "par"))
    vmem = pl.BlockSpec(memory_space=pltpu.VMEM)
    return pl.pallas_call(
        functools.partial(sum_kernel, shards),
        out_shape=jax.ShapeDtypeStruct(packed.shape, jnp.float32),
        in_specs=[vmem],
        out_specs=vmem,
        scratch_shapes=[
            pltpu.VMEM(packed.shape, jnp.float32),
            pltpu.VMEM(packed.shape[1:], jnp.float32),
            pltpu.SemaphoreType.DMA((shards,)),
            pltpu.SemaphoreType.DMA((shards,)),
            pltpu.SemaphoreType.DMA((shards,)),
            pltpu.SemaphoreType.DMA((shards,)),
        ],
        compiler_params=pltpu.CompilerParams(collective_id=0, has_side_effects=True),
    )(packed)


def exact(a, b, dims):
    return lax.dot_general(
        a, b, (dims, ((), ())), precision=lax.Precision.HIGHEST, preferred_element_type=jnp.float32
    )


def transform_kernel(obs_total, x_ref, out_ref, left, right):
    members = out_ref.shape[0]
    scale = 1.0 / obs_total
    line = lax.broadcasted_iota(jnp.int32, (members, members), 0)
    column = lax.broadcasted_iota(jnp.int32, (members, members), 1)
    eye = (line == column).astype(jnp.float32)
    half = members // 2
    parts = x_ref.shape[0]
    size = x_ref.shape[1] - 1
    stacked = jnp.concatenate([x_ref[d, 0:size, :] for d in range(parts)], axis=0)
    gram = jnp.concatenate(
        [
            jnp.concatenate([stacked[0:half], stacked[half:members].T], axis=1),
            jnp.concatenate([stacked[half:members], stacked[members:]], axis=1),
        ],
        axis=0,
    )
    left[...] = gram * scale + eye
    right[...] = eye
    small_line = lax.broadcasted_iota(jnp.int32, (BLOCK, 1), 0)
    small = (
        lax.broadcasted_iota(jnp.int32, (BLOCK, BLOCK), 0) == lax.broadcasted_iota(jnp.int32, (BLOCK, BLOCK), 1)
    ).astype(jnp.float32)
    for b in range(members // BLOCK):
        lo, hi = b * BLOCK, (b + 1) * BLOCK
        a = left[lo:hi, lo:hi]
        x = small
        for j in range(BLOCK):
            factor = a[:, j : j + 1] / a[j : j + 1, j : j + 1]
            factor = jnp.where(small_line > j, factor, 0.0)
            x = x - factor * x[j : j + 1, :]
            a = a - factor * a[j : j + 1, :]
        diagonal = jnp.sum(a * small, axis=1, keepdims=True)
        x = x * lax.rsqrt(diagonal)
        first, later = lo // LANES * LANES, hi // LANES * LANES
        top = -(-hi // LANES) * LANES
        panel_left = exact(x, left[lo:hi, first:], ((1,), (0,)))
        panel_right = exact(x, right[lo:hi, 0:top], ((1,), (0,)))
        right[lo:hi, 0:top] = panel_right
        if hi < members:
            outer = panel_left[:, later - first :]
            update_left = exact(outer, outer, ((0,), (0,)))
            update_right = exact(outer, panel_right, ((0,), (0,)))
            left[hi:, later:] = left[hi:, later:] - update_left[hi - later :, :]
            right[hi:, 0:top] = right[hi:, 0:top] - update_right[hi - later :, :]
    inverse = right[...]
    projection = jnp.concatenate([x_ref[0, size : size + 1, :], x_ref[1, size : size + 1, :]], axis=1) * (
        math.sqrt(members - 1) / obs_total
    )
    half = jnp.sum(inverse * projection, axis=1, keepdims=True)
    weights = exact(inverse, jnp.broadcast_to(half, (members, LANES)), ((0,), (0,)))[:, 0:1]
    out_ref[...] = inverse.T + weights * (1.0 / math.sqrt(members - 1))


def transform_of(total, obs_total):
    members = 2 * total.shape[2]
    return pl.pallas_call(
        functools.partial(transform_kernel, obs_total),
        out_shape=jax.ShapeDtypeStruct((members, members), jnp.float32),
        scratch_shapes=[pltpu.VMEM((members, members), jnp.float32)] * 2,
        compiler_params=pltpu.CompilerParams(vmem_limit_bytes=32 << 20),
    )(total)


def packed_edge(pred, obs):
    high = lax.reduce_precision(obs, 8, 7)
    middle = lax.reduce_precision(obs - high, 8, 7)
    low = obs - high - middle
    parts = jnp.concatenate([high, middle, low, jnp.zeros((EXTRA - 3, H), jnp.float32)], axis=0)
    return jnp.concatenate([pred, parts.astype(jnp.bfloat16)], axis=0)


def body(predicted, observed, band, offsets, rows_count, params):
    members = predicted.shape[0]
    columns = predicted.shape[1]
    axes = ("obs", "par")
    shards = lax.axis_size(axes)
    obs_total = columns * shards
    misfit_factor = math.sqrt((members - 1) / obs_total)
    up = [(i, i + 1) for i in range(shards - 1)]
    down = [(j, i) for i, j in up]
    obs_row = observed[None, :]
    left = lax.ppermute(packed_edge(predicted[:, columns - H :], obs_row[:, columns - H :]), axes, up)
    right = lax.ppermute(packed_edge(predicted[:, :H], obs_row[:, :H]), axes, down)
    acc, row = whiten_gram(
        offsets, rows_count, predicted, left, right, obs_row, band
    )
    total = sum_over_shards(acc, shards)
    transform = transform_of(total, obs_total)
    params_wide = params.astype(jnp.float32)
    param_mean = jnp.mean(params_wide, axis=1, keepdims=True)
    params_new = param_mean + jnp.dot(
        params_wide - param_mean, transform, precision=lax.Precision.HIGHEST
    )
    return (params_new, row[0] * misfit_factor)


def solution(mesh):
    in_specs = (
        P(None, ("grp", "obs", "par")),
        P(("grp", "obs", "par")),
        P(None, ("grp", "obs", "par")),
        P(),
        P(("grp", "obs", "par")),
        P(("grp", "obs", "par"), None),
    )
    out_specs = (P(("grp", "obs", "par"), None), P(("grp", "obs", "par")))
    return jax.shard_map(body, mesh=mesh, in_specs=in_specs, out_specs=out_specs, check_vma=False)
```
